256 devices in a mesh: tok: 64 (over z, y, core), tp: 4 (over x).
Axes of the slice: x: 4, y: 4, z: 8, core: 2. Of those that a mesh axis runs over, the one named last changes fastest.
Arguments:
- attended: bfloat16 [32768, 4096], P('tok', 'tp'), may hold values from -6 to 6
- token_adapter: int32 [32768, 1], P('tok'), may hold values from 0 to 127; in each aligned block of 512 rows (0 to 511, 512 to 1023, ...) at most 6 rows name the same one
- adapter_slot: int32 [128], replicated, may hold values from 0 to 127, each once
- output_weight: bfloat16 [4096, 4096], P('tp'), may hold values from -0.09375 to 0.09375
- adapter_down: bfloat16 [128, 64, 4096], P('tok', None, 'tp'), may hold values from -0.09375 to 0.09375
- adapter_up: bfloat16 [128, 64, 4096], P('tok'), may hold values from -0.75 to 0.75
- block_values: bfloat16 [128, 32, 2, 128, 128], P('tok', 'tp'), may hold values from -0.375 to 0.375
- block_columns: int32 [128, 32, 2], P('tok', 'tp'), may hold values from 0 to 31
Outputs:
- projected: bfloat16 [32768, 4096], P('tok', 'tp')
The draws below stay inside these ranges and needn't reach their ends.
Inputs may be any that keep to these rules, and one draw needn't show every extreme that they name: `token_adapter`: among the 512 tokens of one index of tok, at most 6 name the same adapter; in every draw some adapter is named by exactly 6 tokens of some index of tok. `adapter_slot`: every slot is taken by exactly one adapter.
All inputs are finite; a program needn't handle non-finite values.
Results may differ from the reference program's by a relative error of at most 0.015.
Values may be sent and summed in bfloat16 or wider, within the bound.
No kernel may reach another device: no remote copies, remote signals or barrier semaphores. Data moves between devices by JAX's collectives and lax.ppermute only.
A program may use at most 128 MiB of HBM per device.

```python
import math
import jax
import jax.numpy as jnp
import numpy as np
from jax import lax

D = 4096
EMBED_COLUMNS = 4096
R = 64
BLOCK = 128
BPR = 2
TOK_DEV = 512
ADAPTERS = 128
CAP = 6
TOKENS = 32768
RB = 32
ECB = 32
N_TOK = 64
N_TP = 4


def set_ends(result, stream_key, smallest, high):
    shape = result.shape
    index_at = [jax.random.randint(jax.random.fold_in(stream_key, axis), (), 0, shape[axis]) for axis in range(len(shape))]
    result = result.at[tuple(index_at)].set(smallest)
    longest = shape.index(max(shape))
    index_at[longest] = (index_at[longest] + 1) % shape[longest]
    return result.at[tuple(index_at)].set(high)


def level_of(own_key, extent, cuts, least, largest):
    level = 1.0
    for position, parts in cuts:
        heights = jax.random.uniform(jax.random.fold_in(jax.random.fold_in(own_key, 6), position), (parts,), jnp.float32, least / len(cuts), largest / len(cuts))
        level = level * jnp.repeat(jnp.exp(heights), extent[position] // parts).reshape((-1,) + (1,) * (len(extent) - 1 - position))
    return level


def assign_block(key, own, number, rows, number_of, top, reach, skew):
    order = jax.random.permutation(key, number_of)
    packed, usual = shares(number_of, rows * top, reach, skew, True), shares(number_of, rows * top, reach, skew, False)
    places = jnp.arange(number_of)

    def named(lengths, offset_by):
        used = int((lengths > 0).sum())
        fixed = max(1, used // 4)
        moved = fixed + (places - fixed + offset_by * (used - fixed)) % max(1, number_of - fixed)
        return jnp.zeros((number_of,), jnp.int32).at[order[jnp.where(places < fixed, places, moved)]].set(jnp.asarray(lengths, jnp.int32))

    lengths = jnp.where(number % 4 == 0, named(packed, number // 4), named(usual, number - number // 4 - 1))
    mixed = jax.random.permutation(jax.random.fold_in(own, 3), number_of)
    giver, receiver = mixed[0:number_of // 2 * 2:2], mixed[1:number_of // 2 * 2:2]
    margin = jnp.minimum(lengths[giver] - 1, reach - lengths[receiver]) // 2
    margin = jnp.where((giver == order[0]) | (receiver == order[0]) | (lengths[receiver] == 0), 0, jnp.maximum(margin, 0))
    moved = jax.random.randint(jax.random.fold_in(own, 4), (number_of // 2,), 0, 1 << 20) % (margin + 1)
    lengths = lengths.at[giver].add(-moved).at[receiver].add(moved)
    items = jnp.searchsorted(jnp.cumsum(lengths), jnp.arange(rows * top), side="right").astype(jnp.int32)
    grid = items.reshape(top, rows).T
    grid = grid[jax.random.permutation(jax.random.fold_in(own, 1), rows)]
    offset_by = jax.random.randint(jax.random.fold_in(own, 2), (rows, 1), 0, top)
    return jnp.take_along_axis(grid, (jnp.arange(top)[None, :] + offset_by) % top, axis=1)


def shares(count, total, bound, skew, full):
    loads = [(1 << 20) // math.isqrt(grade ** skew) + 1 for grade in range(1, count + 1)]
    largest = bound if full else min(bound, max(-(-total // count), total * loads[0] // sum(loads)))
    least = 1 if total - largest >= count - 1 else 0
    counts, rest = [largest] + [least] * (count - 1), total - largest - least * (count - 1)
    while rest > 0:
        candidates = [i for i in range(1, count) if counts[i] < largest] or [i for i in range(1, count) if counts[i] < bound]
        whole, remaining = sum([loads[i] for i in candidates]), rest
        for i in candidates:
            more = min(bound - counts[i], max(1, remaining * loads[i] // whole), rest)
            counts[i] = counts[i] + more
            rest = rest - more
    return np.array(counts)


def scatter_about(rng, extent, width, bound, cuts=(), kind=jnp.bfloat16):
    result = jax.random.normal(rng, extent, jnp.float32) * width
    if len(cuts) > 0:
        result = level_of(rng, extent, cuts, -0.22, 0.18) * result
    return jnp.clip(result, min=-bound, max=bound).astype(kind)


def setup_inputs(seed: int = 0) -> dict:
    streams_of = jax.random.split(jax.random.key(seed), 9)
    attended = scatter_about(streams_of[0], (TOKENS, D), 1.0, 6.0, ((0, 64), (1, 4)))
    token_adapter_keys = jax.random.split(jax.random.fold_in(streams_of[1], 1), TOKENS // TOK_DEV)
    token_adapter_turns = jax.random.permutation(jax.random.fold_in(streams_of[1], 3), TOKENS // TOK_DEV)
    token_adapter = jax.vmap(lambda own, number: assign_block(jax.random.fold_in(streams_of[1], 2), own, number, TOK_DEV, ADAPTERS, 1, CAP, 2))(token_adapter_keys, token_adapter_turns).reshape((TOKENS, 1))
    adapter_slot = jax.random.permutation(streams_of[2], ADAPTERS).astype(jnp.int32)
    output_weight = scatter_about(streams_of[3], (D, EMBED_COLUMNS), D ** -0.5, 0.09375, ((0, 4),))
    adapter_down = scatter_about(streams_of[4], (ADAPTERS, R, D), D ** -0.5, 0.09375, ((0, 64), (2, 4)))
    adapter_up = scatter_about(streams_of[5], (ADAPTERS, R, EMBED_COLUMNS), R ** -0.5, 0.75, ((0, 64),))
    block_values = scatter_about(streams_of[6], (ADAPTERS, RB, BPR, BLOCK, BLOCK), (2 * BLOCK) ** -0.5, 0.375, ((0, 64), (1, 4)))
    block_columns = set_ends(jax.random.randint(streams_of[7], (ADAPTERS, RB, BPR), 0, ECB), jax.random.fold_in(streams_of[7], 1), 0, ECB - 1).astype(jnp.int32)
    return dict(attended=attended, token_adapter=token_adapter, adapter_slot=adapter_slot, output_weight=output_weight, adapter_down=adapter_down, adapter_up=adapter_up, block_values=block_values, block_columns=block_columns)


adapter_delta_scale = 2.0


def group_delta(member_rows, down_part, upper_rows, blocks_part, columns_part):
    shrunk = jnp.dot(member_rows, down_part.T, preferred_element_type=jnp.float32).astype(jnp.bfloat16)
    rank_factors = jnp.dot(shrunk, upper_rows, preferred_element_type=jnp.float32)
    count_of_rows = member_rows.shape[0]
    pieces = member_rows.astype(jnp.float32).reshape(count_of_rows, -1, BLOCK)
    block_out = jnp.einsum("nrk,rbkm->nrbm", pieces, blocks_part.astype(jnp.float32), precision=lax.Precision.HIGHEST)
    placement = (columns_part.reshape(-1)[:, None] == jnp.arange(EMBED_COLUMNS // BLOCK, dtype=jnp.int32)[None, :]).astype(jnp.float32)
    sparse_blocks = jnp.einsum("nqm,qe->nem", block_out.reshape(count_of_rows, -1, BLOCK), placement, precision=lax.Precision.HIGHEST)
    return (adapter_delta_scale * rank_factors + sparse_blocks.reshape(count_of_rows, EMBED_COLUMNS)).astype(jnp.bfloat16)


def reference(attended, token_adapter, adapter_slot, output_weight, adapter_down, adapter_up, block_values, block_columns):
    base_part = jnp.dot(attended, output_weight, preferred_element_type=jnp.float32)
    adapter_of = token_adapter[:, 0]
    width_part = D // N_TP
    blocks_group = RB // N_TP
    most_rows = CAP * N_TOK

    def one_adapter(adapter, running):
        slot_index = adapter_slot[adapter]
        members = jnp.nonzero(adapter_of == adapter, size=most_rows, fill_value=TOKENS)[0].astype(jnp.int32)
        member_rows = jnp.take(attended, members, axis=0, mode="fill", fill_value=0)
        down_rows = lax.dynamic_index_in_dim(adapter_down, slot_index, 0, keepdims=False)
        upper_rows = lax.dynamic_index_in_dim(adapter_up, slot_index, 0, keepdims=False)
        blocks_all = lax.dynamic_index_in_dim(block_values, slot_index, 0, keepdims=False)
        columns_all = lax.dynamic_index_in_dim(block_columns, slot_index, 0, keepdims=False)
        joined = jnp.zeros((most_rows, EMBED_COLUMNS), jnp.float32)
        for group_idx in range(N_TP):
            lower = group_idx * width_part
            first_block = group_idx * blocks_group
            part = group_delta(member_rows[:, lower:lower + width_part], down_rows[:, lower:lower + width_part], upper_rows, blocks_all[first_block:first_block + blocks_group], columns_all[first_block:first_block + blocks_group])
            joined = joined + part.astype(jnp.float32)
        return running.at[members].add(joined, mode="drop")

    delta_total = lax.fori_loop(jnp.int32(0), jnp.int32(ADAPTERS), one_adapter, jnp.zeros((TOKENS, EMBED_COLUMNS), jnp.float32))
    return (base_part + delta_total).astype(jnp.bfloat16)
```

```python
import functools

import jax
import jax.numpy as jnp
from jax import lax
from jax.experimental import pallas as pl
from jax.experimental.pallas import tpu as pltpu
from jax.sharding import PartitionSpec as P

BLOCK = 128
CAP = 6
SCALE = 2.0
VMEM = pl.BlockSpec(memory_space=pltpu.VMEM)
SMEM = pl.BlockSpec(memory_space=pltpu.SMEM)
PARAMS = pltpu.CompilerParams(vmem_limit_bytes=40 * 1024 * 1024)
f32, bf16, i32 = jnp.float32, jnp.bfloat16, jnp.int32


def iota(shape, dim):
    return lax.broadcasted_iota(i32, shape, dim)


def dot(a, b, dims=((1,), (0,))):
    return lax.dot_general(a, b, (dims, ((), ())), preferred_element_type=f32)


def pack_kernel(n_tok, n_tp, adapter_ref, slot_ref, x_ref, out_ref, target_ref, wide):
    tokens, width = x_ref.shape
    slots = slot_ref.shape[1]
    pieces = width // BLOCK
    half = CAP // 2
    own_slots = slots // n_tok
    named = (iota((slots, tokens), 0) == adapter_ref[...]).astype(bf16)
    held = (iota((slots, slots), 0) == slot_ref[...]).astype(bf16)
    member = dot(held, named)
    before = (iota((tokens, tokens), 0) < iota((tokens, tokens), 1)).astype(bf16)
    count = dot(member.astype(bf16), before)
    rank = jnp.sum(member * count, axis=0, keepdims=True)
    slot = iota((slots, tokens), 0)
    base = (slot % own_slots) * (2 * n_tok * half) + (slot // own_slots) * half
    start = jnp.sum(member * base.astype(f32), axis=0, keepdims=True)
    place = jnp.where(rank >= half, rank + (n_tok * half - half), rank)
    target = (start + place).astype(i32)
    eye = iota((tokens, tokens), 0) == iota((tokens, tokens), 1)
    target_ref[...] = jnp.sum(jnp.where(eye, target, 0), axis=1, keepdims=True)
    rows = slots * CAP
    pick = (iota((rows, tokens), 0) == target).astype(bf16)
    for j in range(0, pieces, 2):
        both = dot(pick, x_ref[:, j * BLOCK : (j + 2) * BLOCK])
        wide[pl.ds(j, rows, stride=pieces), :] = both[:, :BLOCK]
        wide[pl.ds(j + 1, rows, stride=pieces), :] = both[:, BLOCK:]
    out_ref[...] = wide[...].astype(bf16)


def delta_kernel(groups, meta_ref, x_ref, w_ref, up_ref, out_ref, wide, terms, sums):
    all_rows = x_ref.shape[0]
    rank = up_ref.shape[1]
    columns = up_ref.shape[2] // BLOCK
    per_group = all_rows // groups
    pieces = columns // groups
    rows = per_group // pieces
    slot = meta_ref[0]
    wide[...] = x_ref[...].astype(f32)
    shrunk = jnp.zeros((rows, rank), f32)
    down_at = pieces * 2 * BLOCK
    for g in range(groups):
        for j in range(pieces):
            r = g * pieces + j
            x = wide[pl.ds(g * per_group + j, rows, stride=pieces), :].astype(bf16)
            terms[2 * r] = dot(x, w_ref[g, (2 * j) * BLOCK : (2 * j + 1) * BLOCK, :])
            terms[2 * r + 1] = dot(x, w_ref[g, (2 * j + 1) * BLOCK : (2 * j + 2) * BLOCK, :])
            down = w_ref[g, down_at + j * rank : down_at + (j + 1) * rank, :]
            shrunk = shrunk + dot(x, down, ((1,), (1,)))
    small = (SCALE * shrunk).astype(bf16)
    up = up_ref[slot]
    for c in range(0, columns, 2):
        both = dot(small, up[:, c * BLOCK : (c + 2) * BLOCK])
        sums[c] = both[:, :BLOCK]
        sums[c + 1] = both[:, BLOCK:]
    for q in range(2 * columns):
        c = meta_ref[1 + q]
        sums[c] = sums[c] + terms[q]
    for c in range(columns):
        g, j = divmod(c, pieces)
        wide[pl.ds(g * per_group + j, rows, stride=pieces), :] = sums[c]
    out_ref[...] = wide[...].astype(bf16)


def finish_kernel(target_ref, back_ref, base_ref, out_ref, wide):
    tokens, width = base_ref.shape
    pieces = width // BLOCK
    rows = back_ref.shape[0] // pieces
    wide[...] = back_ref[...].astype(f32)
    pick = (iota((tokens, rows), 1) == target_ref[...]).astype(bf16)
    for j in range(pieces):
        part = wide[pl.ds(j, rows, stride=pieces), :].astype(bf16)
        at = slice(j * BLOCK, (j + 1) * BLOCK)
        out_ref[:, at] = (dot(pick, part) + base_ref[:, at].astype(f32)).astype(bf16)


def cost(flops, moved):
    return pl.CostEstimate(flops=flops, bytes_accessed=moved, transcendentals=0)


def on_device(
    attended,
    token_adapter,
    adapter_slot,
    output_weight,
    adapter_down,
    adapter_up,
    block_values,
    block_columns,
):
    tokens, width = attended.shape
    slots = adapter_slot.shape[0]
    n_tok, n_tp = lax.axis_size("tok"), lax.axis_size("tp")
    own, rank = adapter_down.shape[:2]
    columns = adapter_up.shape[2]
    pieces = width // BLOCK
    lines = slots * CAP * pieces
    share = n_tp // own

    down = jnp.swapaxes(adapter_down.reshape(own, rank, pieces, BLOCK), 1, 2)
    weights = jnp.concatenate(
        [
            block_values.reshape(own, pieces * 2 * BLOCK, BLOCK),
            down.reshape(own, pieces * rank, BLOCK),
        ],
        axis=1,
    )
    weights = jnp.repeat(weights, share, axis=0)
    weights = lax.all_to_all(weights, "tp", 0, 0, tiled=True)
    places = jnp.repeat(block_columns.reshape(own, pieces * 2), share, axis=0)
    places = lax.all_to_all(places, "tp", 0, 0, tiled=True)
    mine = (lax.axis_index("tp") // share).astype(i32)
    meta = jnp.concatenate([mine[None], places.reshape(-1)])

    packed, target = pl.pallas_call(
        functools.partial(pack_kernel, n_tok, n_tp),
        out_shape=(
            jax.ShapeDtypeStruct((lines, BLOCK), bf16),
            jax.ShapeDtypeStruct((tokens, 1), i32),
        ),
        in_specs=[VMEM, VMEM, VMEM],
        out_specs=(VMEM, VMEM),
        scratch_shapes=[pltpu.VMEM((lines, BLOCK), f32)],
        compiler_params=PARAMS,
        cost_estimate=cost(2 * lines // pieces * tokens * width, 6 * lines * BLOCK),
        name="pack_rows",
    )(token_adapter.reshape(1, tokens), adapter_slot.reshape(1, slots), attended)
    came = lax.all_to_all(packed, ("tp", "tok"), 0, 0, tiled=True)

    base = jnp.dot(attended, output_weight, preferred_element_type=f32).astype(bf16)
    base = lax.psum_scatter(base, "tp", scatter_dimension=1, tiled=True)

    rows = lines // pieces // n_tp
    deltas = pl.pallas_call(
        functools.partial(delta_kernel, n_tp),
        out_shape=jax.ShapeDtypeStruct((lines, BLOCK), bf16),
        in_specs=[SMEM, VMEM, VMEM, VMEM],
        out_specs=VMEM,
        scratch_shapes=[
            pltpu.VMEM((lines, BLOCK), f32),
            pltpu.VMEM((2 * columns // BLOCK, rows, BLOCK), f32),
            pltpu.VMEM((columns // BLOCK, rows, BLOCK), f32),
        ],
        compiler_params=PARAMS,
        cost_estimate=cost(6 * rows * columns * 2 * BLOCK, 8 * lines * BLOCK),
        name="slot_deltas",
    )(meta, came, weights, adapter_up)
    back = lax.all_to_all(deltas, ("tp", "tok"), 0, 0, tiled=True)

    return pl.pallas_call(
        finish_kernel,
        out_shape=jax.ShapeDtypeStruct((tokens, width), bf16),
        in_specs=[VMEM, VMEM, VMEM],
        out_specs=VMEM,
        scratch_shapes=[pltpu.VMEM((lines, BLOCK), f32)],
        compiler_params=PARAMS,
        cost_estimate=cost(2 * lines // pieces * tokens * width, 6 * lines * BLOCK),
        name="add_deltas",
    )(target, back, base)


def solution(mesh):
    placed = (
        P("tok", "tp"),
        P("tok", None),
        P(),
        P("tp", None),
        P("tok", None, "tp"),
        P("tok", None, None),
        P("tok", "tp", None, None, None),
        P("tok", "tp", None),
    )
    return jax.shard_map(
        on_device, mesh=mesh, in_specs=placed, out_specs=P("tok", "tp"), check_vma=False
    )
```

```python
import functools

import jax
import jax.numpy as jnp
from jax import lax
from jax.experimental import pallas as pl
from jax.experimental.pallas import tpu as pltpu
from jax.sharding import PartitionSpec as P

BLOCK = 128
CAP = 6
SCALE = 2.0
VMEM = pl.BlockSpec(memory_space=pltpu.VMEM)
SMEM = pl.BlockSpec(memory_space=pltpu.SMEM)
PARAMS = pltpu.CompilerParams(vmem_limit_bytes=40 * 1024 * 1024)
f32, bf16, i32 = jnp.float32, jnp.bfloat16, jnp.int32


def iota(shape, dim):
    return lax.broadcasted_iota(i32, shape, dim)


def dot(a, b, dims=((1,), (0,))):
    return lax.dot_general(a, b, (dims, ((), ())), preferred_element_type=f32)


def pack_kernel(n_tok, n_tp, adapter_ref, slot_ref, x_ref, out_ref, target_ref, wide):
    tokens, width = x_ref.shape
    slots = slot_ref.shape[1]
    pieces = width // BLOCK
    half = CAP // 2
    own_slots = slots // n_tok
    named = (iota((slots, tokens), 0) == adapter_ref[...]).astype(bf16)
    held = (iota((slots, slots), 0) == slot_ref[...]).astype(bf16)
    member = dot(held, named)
    before = (iota((tokens, tokens), 0) < iota((tokens, tokens), 1)).astype(bf16)
    count = dot(member.astype(bf16), before)
    rank = jnp.sum(member * count, axis=0, keepdims=True)
    slot = iota((slots, tokens), 0)
    base = (slot % own_slots) * (2 * n_tok * half) + (slot // own_slots) * half
    start = jnp.sum(member * base.astype(f32), axis=0, keepdims=True)
    place = jnp.where(rank >= half, rank + (n_tok * half - half), rank)
    target = (start + place).astype(i32)
    eye = iota((tokens, tokens), 0) == iota((tokens, tokens), 1)
    target_ref[...] = jnp.sum(jnp.where(eye, target, 0), axis=1, keepdims=True)
    rows = slots * CAP
    pick = (iota((rows, tokens), 0) == target).astype(bf16)
    for j in range(0, pieces, 2):
        both = dot(pick, x_ref[:, j * BLOCK : (j + 2) * BLOCK])
        wide[pl.ds(j, rows, stride=pieces), :] = both[:, :BLOCK]
        wide[pl.ds(j + 1, rows, stride=pieces), :] = both[:, BLOCK:]
    out_ref[...] = wide[...].astype(bf16)


def delta_kernel(groups, at_ref, place_ref, x_ref, up_ref, *refs):
    w_refs, (out_ref, wide, terms, sums) = refs[:groups], refs[groups:]
    all_rows = x_ref.shape[0]
    rank = up_ref.shape[1]
    columns = up_ref.shape[2] // BLOCK
    per_group = all_rows // groups
    pieces = columns // groups
    rows = per_group // pieces
    here, slot = at_ref[0], at_ref[1]
    wide[...] = x_ref[...].astype(f32)
    shrunk = jnp.zeros((rows, rank), f32)
    down_at = pieces * 2 * BLOCK
    for d in range(groups):
        w_ref = w_refs[d]
        g = lax.rem(here + groups - d, groups)
        for j in range(pieces):
            r = d * pieces + j
            x = wide[pl.ds(g * per_group + j, rows, stride=pieces), :].astype(bf16)
            terms[2 * r] = dot(x, w_ref[(2 * j) * BLOCK : (2 * j + 1) * BLOCK, :])
            terms[2 * r + 1] = dot(x, w_ref[(2 * j + 1) * BLOCK : (2 * j + 2) * BLOCK, :])
            down = w_ref[down_at + j * rank : down_at + (j + 1) * rank, :]
            shrunk = shrunk + dot(x, down, ((1,), (1,)))
    small = (SCALE * shrunk).astype(bf16)
    up = up_ref[slot]
    for c in range(0, columns, 2):
        both = dot(small, up[:, c * BLOCK : (c + 2) * BLOCK])
        sums[c] = both[:, :BLOCK]
        sums[c + 1] = both[:, BLOCK:]
    for d in range(groups):
        for q in range(2 * pieces):
            c = place_ref[d * 2 * pieces + q]
            sums[c] = sums[c] + terms[d * 2 * pieces + q]
    for c in range(columns):
        g, j = divmod(c, pieces)
        wide[pl.ds(g * per_group + j, rows, stride=pieces), :] = sums[c]
    out_ref[...] = wide[...].astype(bf16)


def finish_kernel(target_ref, back_ref, base_ref, out_ref, wide):
    tokens, width = base_ref.shape
    pieces = width // BLOCK
    rows = back_ref.shape[0] // pieces
    wide[...] = back_ref[...].astype(f32)
    pick = (iota((tokens, rows), 1) == target_ref[...]).astype(bf16)
    for j in range(pieces):
        part = wide[pl.ds(j, rows, stride=pieces), :].astype(bf16)
        at = slice(j * BLOCK, (j + 1) * BLOCK)
        out_ref[:, at] = (dot(pick, part) + base_ref[:, at].astype(f32)).astype(bf16)


def cost(flops, moved):
    return pl.CostEstimate(flops=flops, bytes_accessed=moved, transcendentals=0)


def on_device(
    attended,
    token_adapter,
    adapter_slot,
    output_weight,
    adapter_down,
    adapter_up,
    block_values,
    block_columns,
):
    tokens, width = attended.shape
    slots = adapter_slot.shape[0]
    n_tok, n_tp = lax.axis_size("tok"), lax.axis_size("tp")
    own, rank = adapter_down.shape[:2]
    columns = adapter_up.shape[2]
    pieces = width // BLOCK
    lines = slots * CAP * pieces
    share = n_tp // own

    packed, target = pl.pallas_call(
        functools.partial(pack_kernel, n_tok, n_tp),
        out_shape=(
            jax.ShapeDtypeStruct((lines, BLOCK), bf16),
            jax.ShapeDtypeStruct((tokens, 1), i32),
        ),
        in_specs=[VMEM, VMEM, VMEM],
        out_specs=(VMEM, VMEM),
        scratch_shapes=[pltpu.VMEM((lines, BLOCK), f32)],
        compiler_params=PARAMS,
        cost_estimate=cost(2 * lines // pieces * tokens * width, 6 * lines * BLOCK),
        name="pack_rows",
    )(token_adapter.reshape(1, tokens), adapter_slot.reshape(1, slots), attended)
    came = lax.all_to_all(packed, ("tp", "tok"), 0, 0, tiled=True)

    here = lax.axis_index("tp")

    packed, adapter_down, block_values, attended = lax.optimization_barrier(
        (packed, adapter_down, block_values, attended)
    )
    spots = block_columns.reshape(own, pieces * 2, 1).astype(bf16)
    down = jnp.swapaxes(adapter_down.reshape(own, rank, pieces, BLOCK), 1, 2)
    held = jnp.concatenate(
        [
            block_values.reshape(own, pieces * 2 * BLOCK, BLOCK),
            down.reshape(own, pieces * rank, BLOCK),
            jnp.broadcast_to(spots, (own, pieces * 2, BLOCK)),
        ],
        axis=1,
    )
    weights = []
    for d in range(n_tp):
        part = lax.dynamic_index_in_dim(held, lax.rem(here + d, n_tp) // share, 0, False)
        if d:
            part = lax.ppermute(part, "tp", [(i, (i + d) % n_tp) for i in range(n_tp)])
        weights.append(part)
    at = jnp.stack([here, here // share]).astype(i32)

    base = jnp.dot(attended, output_weight, preferred_element_type=f32).astype(bf16)
    places = jnp.concatenate([w[-2 * pieces :, 0] for w in weights]).astype(i32)
    base, came, places, *weights = lax.optimization_barrier((base, came, places, *weights))
    base = lax.psum_scatter(base, "tp", scatter_dimension=1, tiled=True)

    rows = lines // pieces // n_tp
    deltas = pl.pallas_call(
        functools.partial(delta_kernel, n_tp),
        out_shape=jax.ShapeDtypeStruct((lines, BLOCK), bf16),
        in_specs=[SMEM, SMEM] + [VMEM] * (2 + n_tp),
        out_specs=VMEM,
        scratch_shapes=[
            pltpu.VMEM((lines, BLOCK), f32),
            pltpu.VMEM((2 * columns // BLOCK, rows, BLOCK), f32),
            pltpu.VMEM((columns // BLOCK, rows, BLOCK), f32),
        ],
        compiler_params=PARAMS,
        cost_estimate=cost(6 * rows * columns * 2 * BLOCK, 8 * lines * BLOCK),
        name="slot_deltas",
    )(at, places, came, adapter_up, *weights)
    back = lax.all_to_all(deltas, ("tp", "tok"), 0, 0, tiled=True)

    return pl.pallas_call(
        finish_kernel,
        out_shape=jax.ShapeDtypeStruct((tokens, width), bf16),
        in_specs=[VMEM, VMEM, VMEM],
        out_specs=VMEM,
        scratch_shapes=[pltpu.VMEM((lines, BLOCK), f32)],
        compiler_params=PARAMS,
        cost_estimate=cost(2 * lines // pieces * tokens * width, 6 * lines * BLOCK),
        name="add_deltas",
    )(target, back, base)


def solution(mesh):
    placed = (
        P("tok", "tp"),
        P("tok", None),
        P(),
        P("tp", None),
        P("tok", None, "tp"),
        P("tok", None, None),
        P("tok", "tp", None, None, None),
        P("tok", "tp", None),
    )
    return jax.shard_map(
        on_device, mesh=mesh, in_specs=placed, out_specs=P("tok", "tp"), check_vma=False
    )
```

```python
import functools

import jax
import jax.numpy as jnp
from jax import lax
from jax.experimental import pallas as pl
from jax.experimental.pallas import tpu as pltpu
from jax.sharding import PartitionSpec as P

BLOCK = 128
CAP = 6
SCALE = 2.0
VMEM = pl.BlockSpec(memory_space=pltpu.VMEM)
SMEM = pl.BlockSpec(memory_space=pltpu.SMEM)
HBM = pl.BlockSpec(memory_space=pltpu.HBM)
PARAMS = pltpu.CompilerParams(vmem_limit_bytes=60 * 1024 * 1024)
f32, bf16, i32 = jnp.float32, jnp.bfloat16, jnp.int32


def iota(shape, dim):
    return lax.broadcasted_iota(i32, shape, dim)


def dot(a, b, dims=((1,), (0,))):
    return lax.dot_general(a, b, (dims, ((), ())), preferred_element_type=f32)


def pack_kernel(n_tok, n_tp, adapter_in, slot_in, x_in, out_ref, target_out, wide, adapter_ref, slot_ref, x_ref, target_ref, sems):
    copies = [
        pltpu.make_async_copy(src, dst, sems.at[i])
        for i, (src, dst) in enumerate(
            ((adapter_in, adapter_ref), (slot_in, slot_ref), (x_in, x_ref))
        )
    ]
    for copy in copies:
        copy.start()
    tokens, width = x_ref.shape
    slots = slot_ref.shape[1]
    pieces = width // BLOCK
    half = CAP // 2
    before = (iota((tokens, tokens), 0) < iota((tokens, tokens), 1)).astype(bf16)
    copies[0].wait()
    copies[1].wait()
    named = (iota((slots, tokens), 0) == adapter_ref[...]).astype(bf16)
    held = (iota((slots, slots), 0) == slot_ref[...]).astype(bf16)
    member = dot(held, named)
    count = dot(member.astype(bf16), before)
    rank = jnp.sum(member * count, axis=0, keepdims=True)
    slot = iota((slots, tokens), 0)
    base = (slot % n_tp) * (n_tok * half) + (slot // n_tp) * CAP
    start = jnp.sum(member * base.astype(f32), axis=0, keepdims=True)
    target = (start + rank).astype(i32)
    target_ref[...] = target
    send_target = pltpu.make_async_copy(target_ref, target_out, sems.at[3])
    send_target.start()
    rows = slots * CAP
    pick = (iota((rows, tokens), 0) == target).astype(bf16)
    copies[2].wait()
    for j in range(0, pieces, 2):
        both = dot(pick, x_ref[:, j * BLOCK : (j + 2) * BLOCK])
        wide[pl.ds(j, rows, stride=pieces), :] = both[:, :BLOCK]
        wide[pl.ds(j + 1, rows, stride=pieces), :] = both[:, BLOCK:]
    out_ref[...] = wide[...].astype(bf16)
    send_target.wait()


def delta_kernel(groups, at_ref, x_in, up_in, other_up_in, *refs):
    given = refs[: 2 * groups]
    out_ref, wide, terms, sums, x_ref, weights, ups, spots, places, sems = refs[2 * groups :]
    here, core, source = at_ref[0], at_ref[1], at_ref[2]
    per_group = x_ref.shape[0] // groups
    shares = [
        pl.ds(pl.multiple_of(lax.rem(here + groups - d, groups) * per_group, per_group), per_group)
        for d in range(groups)
    ]
    x_copies = [
        pltpu.make_async_copy(x_in.at[shares[d]], x_ref.at[pl.ds(d * per_group, per_group)], sems.at[2 * groups + 3 + d])
        for d in range(groups)
    ]
    copies = [
        pltpu.make_async_copy(given[i], weights.at[i], sems.at[i]) for i in range(2 * groups)
    ]
    own, rank, columns = up_in.shape
    up_copies = [
        pltpu.make_async_copy(up_in, ups.at[pl.ds(0, own)], sems.at[2 * groups]),
        pltpu.make_async_copy(other_up_in, ups.at[own], sems.at[2 * groups + 1]),
    ]
    for d in range(groups):
        x_copies[d].start()
        copies[d].start()
        copies[groups + d].start()
    for copy in up_copies:
        copy.start()
    columns = columns // BLOCK
    pieces = columns // groups
    some = pieces // 2
    rows = per_group // pieces
    shrunk = jnp.zeros((rows, rank), f32)
    down_at = pieces * BLOCK
    spots_at = down_at + some * rank

    def piece(d, j):
        return wide[pl.ds(d * per_group + j, rows, stride=pieces), :].astype(bf16)

    for d in range(groups):
        x_copies[d].wait()
        copies[d].wait()
        copies[groups + d].wait()
        own_rows = slice(d * per_group, (d + 1) * per_group)
        wide[own_rows, :] = x_ref[own_rows, :].astype(f32)
        spots[2 * pieces * d : 2 * pieces * (d + 1), :] = (
            weights[d, spots_at : spots_at + 2 * pieces, :].astype(f32).astype(i32)
        )
        for j in range(pieces):
            at = slice(j * BLOCK, (j + 1) * BLOCK)
            pair = jnp.concatenate([weights[d, at, :], weights[groups + d, at, :]], axis=1)
            both = dot(piece(d, j), pair)
            r = d * pieces + j
            terms[2 * r] = both[:, :BLOCK]
            terms[2 * r + 1] = both[:, BLOCK:]
        for j in range(some):
            at = slice(down_at + j * rank, down_at + (j + 1) * rank)
            x = jnp.concatenate([piece(d, core * some + j), piece(d, (1 - core) * some + j)], axis=1)
            down = jnp.concatenate([weights[d, at, :], weights[groups + d, at, :]], axis=1)
            shrunk = shrunk + dot(x, down, ((1,), (1,)))
    to_scalars = pltpu.make_async_copy(spots, places, sems.at[2 * groups + 2])
    to_scalars.start()
    small = (SCALE * shrunk).astype(bf16)
    for copy in up_copies:
        copy.wait()
    for c in range(0, columns, 2):
        both = dot(small, ups[source, :, c * BLOCK : (c + 2) * BLOCK])
        sums[c] = both[:, :BLOCK]
        sums[c + 1] = both[:, BLOCK:]
    to_scalars.wait()
    for r in range(columns):
        c = places[2 * r + core, 0]
        sums[c] = sums[c] + terms[2 * r]
        c = places[2 * r + 1 - core, 0]
        sums[c] = sums[c] + terms[2 * r + 1]
    out_copies = []
    for g in range(groups):
        for j in range(pieces):
            wide[pl.ds(g * per_group + j, rows, stride=pieces), :] = sums[g * pieces + j]
        own_rows = slice(g * per_group, (g + 1) * per_group)
        x_ref[own_rows, :] = wide[own_rows, :].astype(bf16)
        at = pl.ds(g * per_group, per_group)
        copy = pltpu.make_async_copy(x_ref.at[at], out_ref.at[at], sems.at[2 * groups + 3 + g])
        copy.start()
        out_copies.append(copy)
    for copy in out_copies:
        copy.wait()


def finish_kernel(target_in, back_in, base_in, out_ref, wide, target_ref, back_ref, base_ref, sems):
    get_target = pltpu.make_async_copy(target_in, target_ref, sems.at[0])
    get_base = pltpu.make_async_copy(base_in, base_ref, sems.at[1])
    get_back = pltpu.make_async_copy(back_in, back_ref, sems.at[2])
    get_target.start()
    get_back.start()
    get_base.start()
    tokens, width = base_ref.shape
    pieces = width // BLOCK
    rows = back_ref.shape[0] // pieces
    get_target.wait()
    eye = iota((tokens, tokens), 0) == iota((tokens, tokens), 1)
    target = jnp.sum(jnp.where(eye, target_ref[...], 0), axis=1, keepdims=True)
    pick = (iota((tokens, rows), 1) == target).astype(bf16)
    get_back.wait()
    wide[...] = back_ref[...].astype(f32)
    get_base.wait()
    for j in range(0, pieces, 2):
        part = jnp.concatenate(
            [wide[pl.ds(j + i, rows, stride=pieces), :].astype(bf16) for i in range(2)], axis=1
        )
        at = slice(j * BLOCK, (j + 2) * BLOCK)
        out_ref[:, at] = (dot(pick, part) + base_ref[:, at].astype(f32)).astype(bf16)


def cost(flops, moved):
    return pl.CostEstimate(flops=flops, bytes_accessed=moved, transcendentals=0)


def on_device(
    attended,
    token_adapter,
    adapter_slot,
    output_weight,
    adapter_down,
    adapter_up,
    block_values,
    block_columns,
):
    tokens, width = attended.shape
    slots = adapter_slot.shape[0]
    n_tok, n_tp = lax.axis_size("tok"), lax.axis_size("tp")
    own, rank = adapter_down.shape[:2]
    columns = adapter_up.shape[2]
    pieces = width // BLOCK
    lines = slots * CAP * pieces

    packed, target = pl.pallas_call(
        functools.partial(pack_kernel, n_tok, n_tp),
        out_shape=(
            jax.ShapeDtypeStruct((lines, BLOCK), bf16),
            jax.ShapeDtypeStruct((1, tokens), i32),
        ),
        in_specs=[HBM, HBM, HBM],
        out_specs=(VMEM, HBM),
        scratch_shapes=[
            pltpu.VMEM((lines, BLOCK), f32),
            pltpu.VMEM((1, tokens), i32),
            pltpu.VMEM((1, slots), i32),
            pltpu.VMEM((tokens, width), bf16),
            pltpu.VMEM((1, tokens), i32),
            pltpu.SemaphoreType.DMA((4,)),
        ],
        compiler_params=PARAMS,
        cost_estimate=cost(2 * lines // pieces * tokens * width, 6 * lines * BLOCK),
        name="pack_rows",
    )(token_adapter.reshape(1, tokens), adapter_slot.reshape(1, slots), attended)
    came = lax.all_to_all(packed, ("tp", "tok"), 0, 0, tiled=True)

    here, core = lax.axis_index("tp"), lax.axis_index("tok") % 2
    twins = [(i, i ^ 1) for i in range(n_tok)]

    packed, adapter_down, block_values, attended = lax.optimization_barrier(
        (packed, adapter_down, block_values, attended)
    )
    down = jnp.swapaxes(adapter_down.reshape(own, rank, pieces, BLOCK), 1, 2)
    spots = block_columns.reshape(own, pieces * 2, 1).astype(bf16)
    spots = jnp.broadcast_to(spots, (own, pieces * 2, BLOCK))
    halves = jnp.stack(
        [
            jnp.concatenate(
                [
                    block_values[:, :, h].reshape(own, pieces * BLOCK, BLOCK),
                    down[:, h * pieces // 2 : (h + 1) * pieces // 2].reshape(own, -1, BLOCK),
                    spots,
                ],
                axis=1,
            )
            for h in range(2)
        ]
    )
    kept = lax.dynamic_index_in_dim(halves, core, 0, False)
    sent = lax.dynamic_index_in_dim(halves, 1 - core, 0, False)
    got = lax.ppermute(sent, "tok", twins)
    near = []
    for d in range(n_tp):
        s = lax.rem(here + d, n_tp)
        own_part = lax.dynamic_index_in_dim(kept, s % own, 0, False)
        got_part = lax.dynamic_index_in_dim(got, s % own, 0, False)
        part = jnp.where(s // own == core, own_part, got_part)
        if d:
            part = lax.ppermute(part, "tp", [(i, (i + d) % n_tp) for i in range(n_tp)])
        near.append(part)
    base = jnp.dot(attended, output_weight, preferred_element_type=f32).astype(bf16)
    base, *near = lax.optimization_barrier((base, *near))
    far = [lax.ppermute(part, "tok", twins) for part in near]
    other_up = lax.ppermute(
        lax.dynamic_index_in_dim(adapter_up, here % own, 0, False), "tok", twins
    )
    at = jnp.stack([here, core, jnp.where(here // own == core, here % own, own)]).astype(i32)

    held = (base, came, other_up, *near, *far)
    base, came, other_up, *weights = lax.optimization_barrier(held)
    base = lax.psum_scatter(base, "tp", scatter_dimension=1, tiled=True)

    rows = lines // pieces // n_tp
    deltas = pl.pallas_call(
        functools.partial(delta_kernel, n_tp),
        out_shape=jax.ShapeDtypeStruct((lines, BLOCK), bf16),
        in_specs=[SMEM] + [HBM] * (3 + 2 * n_tp),
        out_specs=HBM,
        scratch_shapes=[
            pltpu.VMEM((lines, BLOCK), f32),
            pltpu.VMEM((2 * columns // BLOCK, rows, BLOCK), f32),
            pltpu.VMEM((columns // BLOCK, rows, BLOCK), f32),
            pltpu.VMEM((lines, BLOCK), bf16),
            pltpu.VMEM((2 * n_tp, *near[0].shape), bf16),
            pltpu.VMEM((own + 1, rank, columns), bf16),
            pltpu.VMEM((n_tp * 2 * pieces, BLOCK), i32),
            pltpu.SMEM((n_tp * 2 * pieces, BLOCK), i32),
            pltpu.SemaphoreType.DMA((3 * n_tp + 3,)),
        ],
        compiler_params=PARAMS,
        cost_estimate=cost(6 * rows * columns * 2 * BLOCK, 8 * lines * BLOCK),
        name="slot_deltas",
    )(at, came, adapter_up, other_up, *weights)
    back = lax.all_to_all(deltas, ("tp", "tok"), 0, 0, tiled=True)

    return pl.pallas_call(
        finish_kernel,
        out_shape=jax.ShapeDtypeStruct((tokens, width), bf16),
        in_specs=[HBM, HBM, HBM],
        out_specs=VMEM,
        scratch_shapes=[
            pltpu.VMEM((lines, BLOCK), f32),
            pltpu.VMEM((1, tokens), i32),
            pltpu.VMEM((lines, BLOCK), bf16),
            pltpu.VMEM((tokens, width), bf16),
            pltpu.SemaphoreType.DMA((3,)),
        ],
        compiler_params=PARAMS,
        cost_estimate=cost(2 * lines // pieces * tokens * width, 6 * lines * BLOCK),
        name="add_deltas",
    )(target, back, base)


def solution(mesh):
    placed = (
        P("tok", "tp"),
        P("tok", None),
        P(),
        P("tp", None),
        P("tok", None, "tp"),
        P("tok", None, None),
        P("tok", "tp", None, None, None),
        P("tok", "tp", None),
    )
    return jax.shard_map(
        on_device, mesh=mesh, in_specs=placed, out_specs=P("tok", "tp"), check_vma=False
    )
```

```python
import functools

import jax
import jax.numpy as jnp
from jax import lax
from jax.experimental import pallas as pl
from jax.experimental.pallas import tpu as pltpu
from jax.sharding import Mesh
from jax.sharding import PartitionSpec as P

BLOCK = 128
CAP = 6
SCALE = 2.0
TOK = ("chip", "core")
VMEM = pl.BlockSpec(memory_space=pltpu.VMEM)
SMEM = pl.BlockSpec(memory_space=pltpu.SMEM)
HBM = pl.BlockSpec(memory_space=pltpu.HBM)
PARAMS = pltpu.CompilerParams(vmem_limit_bytes=60 * 1024 * 1024)
f32, bf16, i32 = jnp.float32, jnp.bfloat16, jnp.int32


def iota(shape, dim):
    return lax.broadcasted_iota(i32, shape, dim)


def dot(a, b, dims=((1,), (0,))):
    return lax.dot_general(a, b, (dims, ((), ())), preferred_element_type=f32)


def pack_kernel(n_tok, n_tp, adapter_in, slot_in, x_in, out_ref, target_out, wide, adapter_ref, slot_ref, x_ref, target_ref, sems):
    copies = [
        pltpu.make_async_copy(src, dst, sems.at[i])
        for i, (src, dst) in enumerate(
            ((adapter_in, adapter_ref), (slot_in, slot_ref), (x_in, x_ref))
        )
    ]
    for copy in copies:
        copy.start()
    tokens, width = x_ref.shape
    slots = slot_ref.shape[1]
    pieces = width // BLOCK
    half = CAP // 2
    before = (iota((tokens, tokens), 0) < iota((tokens, tokens), 1)).astype(bf16)
    copies[0].wait()
    copies[1].wait()
    named = (iota((slots, tokens), 0) == adapter_ref[...]).astype(bf16)
    held = (iota((slots, slots), 0) == slot_ref[...]).astype(bf16)
    member = dot(held, named)
    count = dot(member.astype(bf16), before)
    rank = jnp.sum(member * count, axis=0, keepdims=True)
    slot = iota((slots, tokens), 0)
    base = (slot % n_tp) * (n_tok * half) + (slot // n_tp) * CAP
    start = jnp.sum(member * base.astype(f32), axis=0, keepdims=True)
    target = (start + rank).astype(i32)
    target_ref[...] = target
    send_target = pltpu.make_async_copy(target_ref, target_out, sems.at[3])
    send_target.start()
    rows = slots * CAP
    pick = (iota((rows, tokens), 0) == target).astype(bf16)
    copies[2].wait()
    for j in range(0, pieces, 2):
        both = dot(pick, x_ref[:, j * BLOCK : (j + 2) * BLOCK])
        wide[pl.ds(j, rows, stride=pieces), :] = both[:, :BLOCK]
        wide[pl.ds(j + 1, rows, stride=pieces), :] = both[:, BLOCK:]
    out_ref[...] = wide[...].astype(bf16)
    send_target.wait()


def delta_kernel(groups, at_ref, x_in, up_in, other_up_in, *refs):
    given = refs[: 2 * groups]
    out_ref, wide, terms, sums, x_ref, weights, ups, spots, places, sems = refs[2 * groups :]
    here, core, source = at_ref[0], at_ref[1], at_ref[2]
    per_group = x_ref.shape[0] // groups
    shares = [
        pl.ds(pl.multiple_of(lax.rem(here + groups - d, groups) * per_group, per_group), per_group)
        for d in range(groups)
    ]
    x_copies = [
        pltpu.make_async_copy(x_in.at[shares[d]], x_ref.at[pl.ds(d * per_group, per_group)], sems.at[2 * groups + 3 + d])
        for d in range(groups)
    ]
    copies = [
        pltpu.make_async_copy(given[i], weights.at[i], sems.at[i]) for i in range(2 * groups)
    ]
    own, rank, columns = up_in.shape
    up_copies = [
        pltpu.make_async_copy(up_in, ups.at[pl.ds(0, own)], sems.at[2 * groups]),
        pltpu.make_async_copy(other_up_in, ups.at[own], sems.at[2 * groups + 1]),
    ]
    for d in range(groups):
        x_copies[d].start()
        copies[d].start()
        copies[groups + d].start()
    for copy in up_copies:
        copy.start()
    columns = columns // BLOCK
    pieces = columns // groups
    some = pieces // 2
    rows = per_group // pieces
    shrunk = jnp.zeros((rows, rank), f32)
    down_at = pieces * BLOCK
    spots_at = down_at + some * rank

    def piece(d, j):
        return wide[pl.ds(d * per_group + j, rows, stride=pieces), :].astype(bf16)

    for d in range(groups):
        x_copies[d].wait()
        copies[d].wait()
        copies[groups + d].wait()
        own_rows = slice(d * per_group, (d + 1) * per_group)
        wide[own_rows, :] = x_ref[own_rows, :].astype(f32)
        spots[2 * pieces * d : 2 * pieces * (d + 1), :] = (
            weights[d, spots_at : spots_at + 2 * pieces, :].astype(f32).astype(i32)
        )
        for j in range(pieces):
            at = slice(j * BLOCK, (j + 1) * BLOCK)
            pair = jnp.concatenate([weights[d, at, :], weights[groups + d, at, :]], axis=1)
            both = dot(piece(d, j), pair)
            r = d * pieces + j
            terms[2 * r] = both[:, :BLOCK]
            terms[2 * r + 1] = both[:, BLOCK:]
        for j in range(some):
            at = slice(down_at + j * rank, down_at + (j + 1) * rank)
            x = jnp.concatenate([piece(d, core * some + j), piece(d, (1 - core) * some + j)], axis=1)
            down = jnp.concatenate([weights[d, at, :], weights[groups + d, at, :]], axis=1)
            shrunk = shrunk + dot(x, down, ((1,), (1,)))
    to_scalars = pltpu.make_async_copy(spots, places, sems.at[2 * groups + 2])
    to_scalars.start()
    small = (SCALE * shrunk).astype(bf16)
    for copy in up_copies:
        copy.wait()
    for c in range(0, columns, 2):
        both = dot(small, ups[source, :, c * BLOCK : (c + 2) * BLOCK])
        sums[c] = both[:, :BLOCK]
        sums[c + 1] = both[:, BLOCK:]
    to_scalars.wait()
    for r in range(columns):
        c = places[2 * r + core, 0]
        sums[c] = sums[c] + terms[2 * r]
        c = places[2 * r + 1 - core, 0]
        sums[c] = sums[c] + terms[2 * r + 1]
    out_copies = []
    for g in range(groups):
        for j in range(pieces):
            wide[pl.ds(g * per_group + j, rows, stride=pieces), :] = sums[g * pieces + j]
        own_rows = slice(g * per_group, (g + 1) * per_group)
        x_ref[own_rows, :] = wide[own_rows, :].astype(bf16)
        at = pl.ds(g * per_group, per_group)
        copy = pltpu.make_async_copy(x_ref.at[at], out_ref.at[at], sems.at[2 * groups + 3 + g])
        copy.start()
        out_copies.append(copy)
    for copy in out_copies:
        copy.wait()


def base_kernel(chunk_ref, x_ref, w0_ref, w1_ref, *refs):
    half = x_ref.shape[0] // 2
    for i, w_ref in enumerate((w0_ref, w1_ref)):
        total = dot(x_ref[i * half : (i + 1) * half, :], w_ref[...])
        refs[i][...] = total.astype(bf16)


def base_product(chunks, x, w, columns):
    tokens, depth = x.shape
    step = columns // 2
    half = tokens // 2
    part = pl.BlockSpec((half, step), lambda i, c: (0, i))
    return pl.pallas_call(
        base_kernel,
        out_shape=[jax.ShapeDtypeStruct((half, columns), bf16)] * 2,
        grid_spec=pltpu.PrefetchScalarGridSpec(
            num_scalar_prefetch=1,
            grid=(columns // step,),
            in_specs=[
                pl.BlockSpec((tokens, depth), lambda i, c: (0, 0)),
                pl.BlockSpec((depth, step), lambda i, c: (0, c[0] * (columns // step) + i)),
                pl.BlockSpec((depth, step), lambda i, c: (0, c[1] * (columns // step) + i)),
            ],
            out_specs=[part] * 2,
        ),
        compiler_params=PARAMS,
        cost_estimate=cost(2 * tokens * depth * columns, 4 * depth * columns + 6 * tokens * depth),
        name="base_product",
    )(chunks, x, w, w)


def finish_kernel(target_in, back_in, first_in, second_in, mine0_in, mine1_in, out_ref, wide, target_ref, back_ref, base_ref, mine_ref, sems):
    get_target = pltpu.make_async_copy(target_in, target_ref, sems.at[0])
    get_back = pltpu.make_async_copy(back_in, back_ref, sems.at[1])
    half = first_in.shape[0]
    top, bottom = pl.ds(0, half), pl.ds(half, half)
    others = [
        pltpu.make_async_copy(first_in, base_ref.at[top], sems.at[2]),
        pltpu.make_async_copy(second_in, base_ref.at[bottom], sems.at[3]),
        pltpu.make_async_copy(mine0_in, mine_ref.at[top], sems.at[4]),
        pltpu.make_async_copy(mine1_in, mine_ref.at[bottom], sems.at[5]),
    ]
    get_target.start()
    get_back.start()
    for copy in others:
        copy.start()
    tokens, width = base_ref.shape
    pieces = width // BLOCK
    rows = back_ref.shape[0] // pieces
    get_target.wait()
    eye = iota((tokens, tokens), 0) == iota((tokens, tokens), 1)
    target = jnp.sum(jnp.where(eye, target_ref[...], 0), axis=1, keepdims=True)
    pick = (iota((tokens, rows), 1) == target).astype(bf16)
    get_back.wait()
    wide[...] = back_ref[...].astype(f32)
    for copy in others:
        copy.wait()
    for j in range(0, pieces, 2):
        part = jnp.concatenate(
            [wide[pl.ds(j + i, rows, stride=pieces), :].astype(bf16) for i in range(2)], axis=1
        )
        at = slice(j * BLOCK, (j + 2) * BLOCK)
        base = mine_ref[:, at].astype(f32) + base_ref[:, at].astype(f32)
        out_ref[:, at] = (dot(pick, part) + base).astype(bf16)


def cost(flops, moved):
    return pl.CostEstimate(flops=flops, bytes_accessed=moved, transcendentals=0)


def on_device(
    attended,
    token_adapter,
    adapter_slot,
    output_weight,
    adapter_down,
    adapter_up,
    block_values,
    block_columns,
):
    tokens, width = attended.shape
    slots = adapter_slot.shape[0]
    n_tok, n_tp = lax.axis_size(TOK), lax.axis_size("tp")
    own, rank = adapter_down.shape[:2]
    columns = adapter_up.shape[2]
    pieces = width // BLOCK
    lines = slots * CAP * pieces

    packed, target = pl.pallas_call(
        functools.partial(pack_kernel, n_tok, n_tp),
        out_shape=(
            jax.ShapeDtypeStruct((lines, BLOCK), bf16),
            jax.ShapeDtypeStruct((1, tokens), i32),
        ),
        in_specs=[HBM, HBM, HBM],
        out_specs=(VMEM, HBM),
        scratch_shapes=[
            pltpu.VMEM((lines, BLOCK), f32),
            pltpu.VMEM((1, tokens), i32),
            pltpu.VMEM((1, slots), i32),
            pltpu.VMEM((tokens, width), bf16),
            pltpu.VMEM((1, tokens), i32),
            pltpu.SemaphoreType.DMA((4,)),
        ],
        compiler_params=PARAMS,
        cost_estimate=cost(2 * lines // pieces * tokens * width, 6 * lines * BLOCK),
        name="pack_rows",
    )(token_adapter.reshape(1, tokens), adapter_slot.reshape(1, slots), attended)
    came = lax.all_to_all(packed, ("tp", "chip"), 0, 0, tiled=True)

    here, core = lax.axis_index("tp"), lax.axis_index("core")
    onward = [(i, (i + 1) % n_tp) for i in range(n_tp)]
    backward = [(i, (i - 1) % n_tp) for i in range(n_tp)]
    twins = [(0, 1), (1, 0)]

    def ring_step(parts):
        return [lax.ppermute(parts[0], "tp", onward), lax.ppermute(parts[1], "tp", backward)]

    def product(offset, x):
        chunks = lax.rem(jnp.stack([here + n_tp - offset, here + offset]), n_tp).astype(i32)
        return base_product(chunks, x, output_weight, width)

    def added(parts, more):
        return [(a.astype(f32) + b.astype(f32)).astype(bf16) for a, b in zip(parts, more)]

    packed, adapter_down, block_values, x = lax.optimization_barrier(
        (packed, adapter_down, block_values, attended)
    )

    down = jnp.swapaxes(adapter_down.reshape(own, rank, pieces, BLOCK), 1, 2)
    spots = block_columns.reshape(own, pieces * 2, 1).astype(bf16)
    spots = jnp.broadcast_to(spots, (own, pieces * 2, BLOCK))
    halves = jnp.stack(
        [
            jnp.concatenate(
                [
                    block_values[:, :, h].reshape(own, pieces * BLOCK, BLOCK),
                    down[:, h * pieces // 2 : (h + 1) * pieces // 2].reshape(own, -1, BLOCK),
                    spots,
                ],
                axis=1,
            )
            for h in range(2)
        ]
    )
    kept = lax.dynamic_index_in_dim(halves, core, 0, False)
    sent = lax.dynamic_index_in_dim(halves, 1 - core, 0, False)
    got = lax.ppermute(sent, "core", twins)
    other_up = lax.ppermute(
        lax.dynamic_index_in_dim(adapter_up, here % own, 0, False), "core", twins
    )
    near = []
    for d in range(n_tp):
        s = lax.rem(here + d, n_tp)
        own_part = lax.dynamic_index_in_dim(kept, s % own, 0, False)
        got_part = lax.dynamic_index_in_dim(got, s % own, 0, False)
        near.append(jnp.where(s // own == core, own_part, got_part))
    *near, other_up, x = lax.optimization_barrier((*near, other_up, x))
    for d in range(1, n_tp):
        near[d] = lax.ppermute(near[d], "tp", [(i, (i + d) % n_tp) for i in range(n_tp)])
    products = [y for offset in (1, 2, 3, 0) for y in product(offset, x)]
    held = lax.optimization_barrier((*near, *products))
    near, products = held[:n_tp], held[n_tp:]
    far = [lax.ppermute(part, "core", twins) for part in near]
    at = jnp.stack([here, core, jnp.where(here // own == core, here % own, own)]).astype(i32)
    came, *weights = lax.optimization_barrier((came, *near, *far))

    rows = lines // pieces // n_tp
    deltas = pl.pallas_call(
        functools.partial(delta_kernel, n_tp),
        out_shape=jax.ShapeDtypeStruct((lines, BLOCK), bf16),
        in_specs=[SMEM] + [HBM] * (3 + 2 * n_tp),
        out_specs=HBM,
        scratch_shapes=[
            pltpu.VMEM((lines, BLOCK), f32),
            pltpu.VMEM((2 * columns // BLOCK, rows, BLOCK), f32),
            pltpu.VMEM((columns // BLOCK, rows, BLOCK), f32),
            pltpu.VMEM((lines, BLOCK), bf16),
            pltpu.VMEM((2 * n_tp, *near[0].shape), bf16),
            pltpu.VMEM((own + 1, rank, columns), bf16),
            pltpu.VMEM((n_tp * 2 * pieces, BLOCK), i32),
            pltpu.SMEM((n_tp * 2 * pieces, BLOCK), i32),
            pltpu.SemaphoreType.DMA((3 * n_tp + 3,)),
        ],
        compiler_params=PARAMS,
        cost_estimate=cost(6 * rows * columns * 2 * BLOCK, 8 * lines * BLOCK),
        name="slot_deltas",
    )(at, came, adapter_up, other_up, *weights)
    sums = ring_step(products[:2])
    deltas, *sums = lax.optimization_barrier((deltas, *sums))
    sums = ring_step(added(sums, products[2:4]))
    sums = ring_step(added(sums, products[4:6]))
    back = lax.all_to_all(deltas, ("tp", "chip"), 0, 0, tiled=True)

    return pl.pallas_call(
        finish_kernel,
        out_shape=jax.ShapeDtypeStruct((tokens, width), bf16),
        in_specs=[HBM] * 6,
        out_specs=VMEM,
        scratch_shapes=[
            pltpu.VMEM((lines, BLOCK), f32),
            pltpu.VMEM((1, tokens), i32),
            pltpu.VMEM((lines, BLOCK), bf16),
            pltpu.VMEM((tokens, width), bf16),
            pltpu.VMEM((tokens, width), bf16),
            pltpu.SemaphoreType.DMA((6,)),
        ],
        compiler_params=PARAMS,
        cost_estimate=cost(2 * lines // pieces * tokens * width, 6 * lines * BLOCK),
        name="add_deltas",
    )(target, back, *sums, *products[6:])


def solution(mesh):
    placed = (
        P(TOK, "tp"),
        P(TOK, None),
        P(),
        P("tp", None),
        P(TOK, None, "tp"),
        P(TOK, None, None),
        P(TOK, "tp", None, None, None),
        P(TOK, "tp", None),
    )
    mesh = Mesh(mesh.devices.reshape(-1, 2, mesh.shape["tp"]), (*TOK, "tp"))
    return jax.shard_map(
        on_device, mesh=mesh, in_specs=placed, out_specs=P(TOK, "tp"), check_vma=False
    )
```

```python
import functools

import jax
import jax.numpy as jnp
from jax import lax
from jax.experimental import pallas as pl
from jax.experimental.pallas import tpu as pltpu
from jax.sharding import Mesh
from jax.sharding import PartitionSpec as P

BLOCK = 128
CAP = 6
SCALE = 2.0
TOK = ("chip", "core")
VMEM = pl.BlockSpec(memory_space=pltpu.VMEM)
SMEM = pl.BlockSpec(memory_space=pltpu.SMEM)
HBM = pl.BlockSpec(memory_space=pltpu.HBM)
PARAMS = pltpu.CompilerParams(vmem_limit_bytes=60 * 1024 * 1024)
f32, bf16, i32 = jnp.float32, jnp.bfloat16, jnp.int32


def iota(shape, dim):
    return lax.broadcasted_iota(i32, shape, dim)


def dot(a, b, dims=((1,), (0,))):
    return lax.dot_general(a, b, (dims, ((), ())), preferred_element_type=f32)


def pack_kernel(n_tok, n_tp, adapter_in, slot_in, x_in, out_ref, target_out, wide, adapter_ref, slot_ref, x_ref, target_ref, packed_ref, sems):
    copies = [
        pltpu.make_async_copy(src, dst, sems.at[i])
        for i, (src, dst) in enumerate(
            ((adapter_in, adapter_ref), (slot_in, slot_ref), (x_in, x_ref))
        )
    ]
    for copy in copies:
        copy.start()
    tokens, width = x_ref.shape
    slots = slot_ref.shape[1]
    pieces = width // BLOCK
    half = CAP // 2
    before = (iota((tokens, tokens), 0) < iota((tokens, tokens), 1)).astype(bf16)
    copies[0].wait()
    copies[1].wait()
    named = (iota((slots, tokens), 0) == adapter_ref[...]).astype(bf16)
    held = (iota((slots, slots), 0) == slot_ref[...]).astype(bf16)
    member = dot(held, named)
    count = dot(member.astype(bf16), before)
    rank = jnp.sum(member * count, axis=0, keepdims=True)
    slot = iota((slots, tokens), 0)
    base = (slot % n_tp) * (n_tok * half) + (slot // n_tp) * CAP
    start = jnp.sum(member * base.astype(f32), axis=0, keepdims=True)
    target = (start + rank).astype(i32)
    target_ref[...] = target
    send_target = pltpu.make_async_copy(target_ref, target_out, sems.at[3])
    send_target.start()
    rows = slots * CAP
    some = rows // n_tp
    copies[2].wait()
    sends = []
    for g in range(n_tp):
        pick = (iota((some, tokens), 0) + g * some == target).astype(bf16)
        first = g * some * pieces
        for j in range(0, pieces, 2):
            both = dot(pick, x_ref[:, j * BLOCK : (j + 2) * BLOCK])
            wide[pl.ds(first + j, some, stride=pieces), :] = both[:, :BLOCK]
            wide[pl.ds(first + j + 1, some, stride=pieces), :] = both[:, BLOCK:]
        at = pl.ds(first, some * pieces)
        packed_ref[at, :] = wide[at, :].astype(bf16)
        sends.append(pltpu.make_async_copy(packed_ref.at[at], out_ref.at[at], sems.at[4 + g]))
        sends[-1].start()
    for copy in (send_target, *sends):
        copy.wait()


def delta_kernel(groups, at_ref, x_in, up_in, other_up_in, *refs):
    given = refs[: 2 * groups]
    out_ref, wide, terms, sums, x_ref, weights, ups, spots, places, sems = refs[2 * groups :]
    here, core, source = at_ref[0], at_ref[1], at_ref[2]
    per_group = x_ref.shape[0] // groups
    shares = [
        pl.ds(pl.multiple_of(lax.rem(here + groups - d, groups) * per_group, per_group), per_group)
        for d in range(groups)
    ]
    x_copies = [
        pltpu.make_async_copy(x_in.at[shares[d]], x_ref.at[pl.ds(d * per_group, per_group)], sems.at[2 * groups + 3 + d])
        for d in range(groups)
    ]
    copies = [
        pltpu.make_async_copy(given[i], weights.at[i], sems.at[i]) for i in range(2 * groups)
    ]
    own, rank, columns = up_in.shape
    up_copies = [
        pltpu.make_async_copy(up_in, ups.at[pl.ds(0, own)], sems.at[2 * groups]),
        pltpu.make_async_copy(other_up_in, ups.at[own], sems.at[2 * groups + 1]),
    ]
    for d in range(groups):
        x_copies[d].start()
        copies[d].start()
        copies[groups + d].start()
    for copy in up_copies:
        copy.start()
    columns = columns // BLOCK
    pieces = columns // groups
    some = pieces // 2
    rows = per_group // pieces
    shrunk = jnp.zeros((rows, rank), f32)
    down_at = pieces * BLOCK
    spots_at = down_at + some * rank

    def piece(d, j):
        return wide[pl.ds(d * per_group + j, rows, stride=pieces), :].astype(bf16)

    for d in range(groups):
        x_copies[d].wait()
        copies[d].wait()
        copies[groups + d].wait()
        own_rows = slice(d * per_group, (d + 1) * per_group)
        wide[own_rows, :] = x_ref[own_rows, :].astype(f32)
        spots[2 * pieces * d : 2 * pieces * (d + 1), :] = (
            weights[d, spots_at : spots_at + 2 * pieces, :].astype(f32).astype(i32)
        )
        for j in range(pieces):
            at = slice(j * BLOCK, (j + 1) * BLOCK)
            pair = jnp.concatenate([weights[d, at, :], weights[groups + d, at, :]], axis=1)
            both = dot(piece(d, j), pair)
            r = d * pieces + j
            terms[2 * r] = both[:, :BLOCK]
            terms[2 * r + 1] = both[:, BLOCK:]
        for j in range(some):
            at = slice(down_at + j * rank, down_at + (j + 1) * rank)
            x = jnp.concatenate([piece(d, core * some + j), piece(d, (1 - core) * some + j)], axis=1)
            down = jnp.concatenate([weights[d, at, :], weights[groups + d, at, :]], axis=1)
            shrunk = shrunk + dot(x, down, ((1,), (1,)))
    to_scalars = pltpu.make_async_copy(spots, places, sems.at[2 * groups + 2])
    to_scalars.start()
    small = (SCALE * shrunk).astype(bf16)
    for copy in up_copies:
        copy.wait()
    for c in range(0, columns, 2):
        both = dot(small, ups[source, :, c * BLOCK : (c + 2) * BLOCK])
        sums[c] = both[:, :BLOCK]
        sums[c + 1] = both[:, BLOCK:]
    to_scalars.wait()
    for r in range(columns):
        c = places[2 * r + core, 0]
        sums[c] = sums[c] + terms[2 * r]
        c = places[2 * r + 1 - core, 0]
        sums[c] = sums[c] + terms[2 * r + 1]
    out_copies = []
    for g in range(groups):
        for j in range(pieces):
            wide[pl.ds(g * per_group + j, rows, stride=pieces), :] = sums[g * pieces + j]
        own_rows = slice(g * per_group, (g + 1) * per_group)
        x_ref[own_rows, :] = wide[own_rows, :].astype(bf16)
        at = pl.ds(g * per_group, per_group)
        copy = pltpu.make_async_copy(x_ref.at[at], out_ref.at[at], sems.at[2 * groups + 3 + g])
        copy.start()
        out_copies.append(copy)
    for copy in out_copies:
        copy.wait()


def base_kernel(chunk_ref, x_ref, w_ref, top_ref, bottom_ref):
    half = top_ref.shape[0]
    total = dot(x_ref[...], w_ref[...]).astype(bf16)
    top_ref[...] = total[:half]
    bottom_ref[...] = total[half:]


def base_product(chunk, x, w, columns):
    tokens, depth = x.shape
    step = columns // 2
    half = tokens // 2
    part = pl.BlockSpec((half, step), lambda i, c: (0, i))
    return pl.pallas_call(
        base_kernel,
        out_shape=[jax.ShapeDtypeStruct((half, columns), bf16)] * 2,
        grid_spec=pltpu.PrefetchScalarGridSpec(
            num_scalar_prefetch=1,
            grid=(columns // step,),
            in_specs=[
                pl.BlockSpec((tokens, depth), lambda i, c: (0, 0)),
                pl.BlockSpec((depth, step), lambda i, c: (0, c[0] * (columns // step) + i)),
            ],
            out_specs=[part] * 2,
        ),
        compiler_params=PARAMS,
        cost_estimate=cost(2 * tokens * depth * columns, 2 * depth * columns + 4 * tokens * depth),
        name="base_product",
    )(chunk, x, w)


def finish_kernel(target_in, back_in, *refs):
    terms, (out_ref, wide, target_ref, back_ref, base_ref, sems) = refs[:6], refs[6:]
    get_target = pltpu.make_async_copy(target_in, target_ref, sems.at[0])
    get_back = pltpu.make_async_copy(back_in, back_ref, sems.at[1])
    half = terms[0].shape[0]
    others = [
        pltpu.make_async_copy(
            terms[2 * i + j], base_ref.at[i, pl.ds(j * half, half)], sems.at[2 + 2 * i + j]
        )
        for i in range(3)
        for j in range(2)
    ]
    get_target.start()
    get_back.start()
    for copy in others:
        copy.start()
    tokens, width = base_ref.shape[1:]
    pieces = width // BLOCK
    rows = back_ref.shape[0] // pieces
    get_target.wait()
    eye = iota((tokens, tokens), 0) == iota((tokens, tokens), 1)
    target = jnp.sum(jnp.where(eye, target_ref[...], 0), axis=1, keepdims=True)
    pick = (iota((tokens, rows), 1) == target).astype(bf16)
    get_back.wait()
    wide[...] = back_ref[...].astype(f32)
    for copy in others:
        copy.wait()
    for j in range(0, pieces, 2):
        part = jnp.concatenate(
            [wide[pl.ds(j + i, rows, stride=pieces), :].astype(bf16) for i in range(2)], axis=1
        )
        at = slice(j * BLOCK, (j + 2) * BLOCK)
        base = base_ref[0, :, at].astype(f32) + base_ref[1, :, at].astype(f32) + base_ref[2, :, at].astype(f32)
        out_ref[:, at] = (dot(pick, part) + base).astype(bf16)


def cost(flops, moved):
    return pl.CostEstimate(flops=flops, bytes_accessed=moved, transcendentals=0)


def on_device(
    attended,
    token_adapter,
    adapter_slot,
    output_weight,
    adapter_down,
    adapter_up,
    block_values,
    block_columns,
):
    tokens, width = attended.shape
    slots = adapter_slot.shape[0]
    n_tok, n_tp = lax.axis_size(TOK), lax.axis_size("tp")
    own, rank = adapter_down.shape[:2]
    columns = adapter_up.shape[2]
    pieces = width // BLOCK
    lines = slots * CAP * pieces

    packed, target = pl.pallas_call(
        functools.partial(pack_kernel, n_tok, n_tp),
        out_shape=(
            jax.ShapeDtypeStruct((lines, BLOCK), bf16),
            jax.ShapeDtypeStruct((1, tokens), i32),
        ),
        in_specs=[HBM, HBM, HBM],
        out_specs=(HBM, HBM),
        scratch_shapes=[
            pltpu.VMEM((lines, BLOCK), f32),
            pltpu.VMEM((1, tokens), i32),
            pltpu.VMEM((1, slots), i32),
            pltpu.VMEM((tokens, width), bf16),
            pltpu.VMEM((1, tokens), i32),
            pltpu.VMEM((lines, BLOCK), bf16),
            pltpu.SemaphoreType.DMA((4 + n_tp,)),
        ],
        compiler_params=PARAMS,
        cost_estimate=cost(2 * lines // pieces * tokens * width, 6 * lines * BLOCK),
        name="pack_rows",
    )(token_adapter.reshape(1, tokens), adapter_slot.reshape(1, slots), attended)
    came = lax.all_to_all(packed, ("tp", "chip"), 0, 0, tiled=True)

    here, core = lax.axis_index("tp"), lax.axis_index("core")
    onward = [(i, (i + 1) % n_tp) for i in range(n_tp)]
    backward = [(i, (i - 1) % n_tp) for i in range(n_tp)]
    twins = [(0, 1), (1, 0)]

    def product(offset, x):
        chunk = lax.rem(here + offset, n_tp).astype(i32)[None]
        return base_product(chunk, x, output_weight, width)

    def added(a, b):
        return (a.astype(f32) + b.astype(f32)).astype(bf16)

    packed, adapter_down, block_values, x = lax.optimization_barrier(
        (packed, adapter_down, block_values, attended)
    )

    down = jnp.swapaxes(adapter_down.reshape(own, rank, pieces, BLOCK), 1, 2)
    spots = block_columns.reshape(own, pieces * 2, 1).astype(bf16)
    spots = jnp.broadcast_to(spots, (own, pieces * 2, BLOCK))
    halves = jnp.stack(
        [
            jnp.concatenate(
                [
                    block_values[:, :, h].reshape(own, pieces * BLOCK, BLOCK),
                    down[:, h * pieces // 2 : (h + 1) * pieces // 2].reshape(own, -1, BLOCK),
                    spots,
                ],
                axis=1,
            )
            for h in range(2)
        ]
    )
    kept = lax.dynamic_index_in_dim(halves, core, 0, False)
    sent = lax.dynamic_index_in_dim(halves, 1 - core, 0, False)
    got = lax.ppermute(sent, "core", twins)
    other_up = lax.ppermute(
        lax.dynamic_index_in_dim(adapter_up, here % own, 0, False), "core", twins
    )
    near = []
    for d in range(n_tp):
        s = lax.rem(here + d, n_tp)
        own_part = lax.dynamic_index_in_dim(kept, s % own, 0, False)
        got_part = lax.dynamic_index_in_dim(got, s % own, 0, False)
        near.append(jnp.where(s // own == core, own_part, got_part))
    *near, other_up, x = lax.optimization_barrier((*near, other_up, x))
    for d in range(1, n_tp):
        near[d] = lax.ppermute(near[d], "tp", [(i, (i + d) % n_tp) for i in range(n_tp)])
    products = [y for offset in (2, 1, 3, 0) for y in product(offset, x)]
    held = lax.optimization_barrier((*near, *products))
    near, products = held[:n_tp], held[n_tp:]
    far = [lax.ppermute(part, "core", twins) for part in near]
    at = jnp.stack([here, core, jnp.where(here // own == core, here % own, own)]).astype(i32)
    came, *weights = lax.optimization_barrier((came, *near, *far))

    rows = lines // pieces // n_tp
    deltas = pl.pallas_call(
        functools.partial(delta_kernel, n_tp),
        out_shape=jax.ShapeDtypeStruct((lines, BLOCK), bf16),
        in_specs=[SMEM] + [HBM] * (3 + 2 * n_tp),
        out_specs=HBM,
        scratch_shapes=[
            pltpu.VMEM((lines, BLOCK), f32),
            pltpu.VMEM((2 * columns // BLOCK, rows, BLOCK), f32),
            pltpu.VMEM((columns // BLOCK, rows, BLOCK), f32),
            pltpu.VMEM((lines, BLOCK), bf16),
            pltpu.VMEM((2 * n_tp, *near[0].shape), bf16),
            pltpu.VMEM((own + 1, rank, columns), bf16),
            pltpu.VMEM((n_tp * 2 * pieces, BLOCK), i32),
            pltpu.SMEM((n_tp * 2 * pieces, BLOCK), i32),
            pltpu.SemaphoreType.DMA((3 * n_tp + 3,)),
        ],
        compiler_params=PARAMS,
        cost_estimate=cost(6 * rows * columns * 2 * BLOCK, 8 * lines * BLOCK),
        name="slot_deltas",
    )(at, came, adapter_up, other_up, *weights)
    far_top, far_bottom, next_top, next_bottom, last_top, last_bottom, *mine = products
    via_last = lax.ppermute(far_top, "tp", onward)
    via_next = lax.ppermute(far_bottom, "tp", backward)
    deltas, via_last, via_next = lax.optimization_barrier((deltas, via_last, via_next))
    sums = [
        lax.ppermute(added(next_top, via_last), "tp", onward),
        lax.ppermute(next_bottom, "tp", onward),
        lax.ppermute(last_top, "tp", backward),
        lax.ppermute(added(last_bottom, via_next), "tp", backward),
    ]
    back = lax.all_to_all(deltas, ("tp", "chip"), 0, 0, tiled=True)

    return pl.pallas_call(
        finish_kernel,
        out_shape=jax.ShapeDtypeStruct((tokens, width), bf16),
        in_specs=[HBM] * 8,
        out_specs=VMEM,
        scratch_shapes=[
            pltpu.VMEM((lines, BLOCK), f32),
            pltpu.VMEM((1, tokens), i32),
            pltpu.VMEM((lines, BLOCK), bf16),
            pltpu.VMEM((3, tokens, width), bf16),
            pltpu.SemaphoreType.DMA((8,)),
        ],
        compiler_params=PARAMS,
        cost_estimate=cost(2 * lines // pieces * tokens * width, 6 * lines * BLOCK),
        name="add_deltas",
    )(target, back, *sums, *mine)


def solution(mesh):
    placed = (
        P(TOK, "tp"),
        P(TOK, None),
        P(),
        P("tp", None),
        P(TOK, None, "tp"),
        P(TOK, None, None),
        P(TOK, "tp", None, None, None),
        P(TOK, "tp", None),
    )
    mesh = Mesh(mesh.devices.reshape(-1, 2, mesh.shape["tp"]), (*TOK, "tp"))
    return jax.shard_map(
        on_device, mesh=mesh, in_specs=placed, out_specs=P(TOK, "tp"), check_vma=False
    )
```
